32 devices in a mesh: groups: 2 (over x), dp: 16 (over z, y, core).
Axes of the slice: x: 2, y: 2, z: 4, core: 2. Of those that a mesh axis runs over, the one named last changes fastest.
Arguments:
- inputs: bfloat16 [4096, 8192], P(('groups', 'dp')), parts along dimension 0, may hold values from -6 to 6
- output_gradient: bfloat16 [4096, 1024], P(('groups', 'dp')), parts along dimension 0, may hold values from -6 to 6
- token_adapter_index: int32 [4096, 1], P(('groups', 'dp')), parts along dimension 0, may hold values from 0 to 15; in each aligned block of 128 rows (0 to 127, 128 to 255, ...) at most 12 rows name the same one
- owner_index_map: int32 [16], replicated, may hold values from 0 to 15, each once
- frozen_key_weight: bfloat16 [8192, 1024], P('dp'), may hold values from -0.0625 to 0.0625
- down_panels: bfloat16 [16, 8192, 64], P('dp'), may hold values from -0.0625 to 0.0625
- up_panels: bfloat16 [16, 64, 1024], P('dp'), may hold values from -0.1875 to 0.1875
Outputs:
- input_gradient: bfloat16 [4096, 8192], P(('groups', 'dp')), parts along dimension 0
- down_panel_gradient: float32 [32, 8192, 64], P(('groups', 'dp')), parts along dimension 0
- up_panel_gradient: float32 [32, 64, 1024], P(('groups', 'dp')), parts along dimension 0
The draws below stay inside these ranges and needn't reach their ends.
There are 2 independent parts, one for each index of `groups`. The reference program is written for one: setup_inputs(seed, part) draws one part's arguments, and reference() takes and returns one part's arrays. A program takes and returns all parts, laid end to end along the dimension named above; an argument that names none is the same for every part. Nothing has to cross between parts.
Inputs may be any that keep to these rules, and one draw needn't show every extreme that they name: `token_adapter_index`: within the rows of one index of dp no adapter appears more than 12 times, and some adapter appears exactly 12 times there. `owner_index_map`: every index of dp owns exactly one adapter.
All inputs are finite; a program needn't handle non-finite values.
Results may differ from the reference program's by a relative error of at most 0.0042.
Values may be sent and summed in bfloat16 or wider, within the bound.
A program may use at most 128 MiB of HBM per device.

```python
import math
import jax
import jax.numpy as jnp
import numpy as np
from jax import lax

MODEL_WIDTH = 8192
KEY_WIDTH = 1024
ADAPTER_RANK = 64
TOK_DEV = 128
ADAPTER_TOTAL = 16
TOKENS = 2048
CAP = 12
N_DP = 16


def level_of(key, dims, shards, smallest, largest):
    def one(dim, blocks):
        heights = jax.random.uniform(jax.random.fold_in(jax.random.fold_in(key, 6), dim), (blocks,), jnp.float32, smallest / len(shards), largest / len(shards))
        return jnp.repeat(jnp.exp(heights), dims[dim] // blocks).reshape((-1,) + (1,) * (len(dims) - dim - 1))

    loudness = one(*shards[0])
    for cut in shards[1:]:
        loudness = loudness * one(*cut)
    return loudness


def deal_out(rng, own, number, rows, amount, top, most, lean):
    sequence = jax.random.permutation(rng, amount)
    heavy_load, usual = load_shares(amount, rows * top, most, lean, True), load_shares(amount, rows * top, most, lean, False)
    places = jnp.arange(amount)

    def named(tallies, turn):
        used = int((tallies > 0).sum())
        fixed = max(1, used // 4)
        shifted = fixed + (places - fixed + turn * (used - fixed)) % max(1, amount - fixed)
        return jnp.zeros((amount,), jnp.int32).at[sequence[jnp.where(places < fixed, places, shifted)]].set(jnp.asarray(tallies, jnp.int32))

    tallies = jnp.where(number % 4 == 0, named(heavy_load, number // 4), named(usual, number - number // 4 - 1))
    mixed = jax.random.permutation(jax.random.fold_in(own, 3), amount)
    giver, receiver = mixed[0:amount // 2 * 2:2], mixed[1:amount // 2 * 2:2]
    margin = jnp.minimum(tallies[giver] - 1, most - tallies[receiver]) // 2
    margin = jnp.where((giver == sequence[0]) | (receiver == sequence[0]) | (tallies[receiver] == 0), 0, jnp.maximum(margin, 0))
    shifted = jax.random.randint(jax.random.fold_in(own, 4), (amount // 2,), 0, 1 << 20) % (margin + 1)
    tallies = tallies.at[giver].add(-shifted).at[receiver].add(shifted)
    items = jnp.searchsorted(jnp.cumsum(tallies), jnp.arange(rows * top), side="right").astype(jnp.int32)
    listing = items.reshape(top, rows).T
    listing = listing[jax.random.permutation(jax.random.fold_in(own, 1), rows)]
    turn = jax.random.randint(jax.random.fold_in(own, 2), (rows, 1), 0, top)
    return jnp.take_along_axis(listing, (jnp.arange(top)[None, :] + turn) % top, axis=1)


def load_shares(number_of, total, bound, skew, full):
    portions = [(1 << 20) // math.isqrt(grade ** skew) + 1 for grade in range(1, number_of + 1)]
    largest = bound if full else min(bound, max(-(-total // number_of), total * portions[0] // sum(portions)))
    least = 1 if total - largest >= number_of - 1 else 0
    holding, rest = [largest] + [least] * (number_of - 1), total - largest - least * (number_of - 1)
    while rest > 0:
        candidates = [i for i in range(1, number_of) if holding[i] < largest] or [i for i in range(1, number_of) if holding[i] < bound]
        pool, budget = sum([portions[i] for i in candidates]), rest
        for i in candidates:
            addition = min(bound - holding[i], max(1, budget * portions[i] // pool), rest)
            holding[i] = holding[i] + addition
            rest = rest - addition
    return np.array(holding)


def noise(own_key, dims, spread, reach, shards=(), kind=jnp.bfloat16):
    drawn = jax.random.normal(own_key, dims, jnp.float32) * spread
    if len(shards) > 0:
        drawn = level_of(own_key, dims, shards, -0.22, 0.18) * drawn
    return jnp.clip(drawn, min=-reach, max=reach).astype(kind)


def setup_inputs(seed: int = 0, part: int = 0) -> dict:
    key_of = jax.random.split(jax.random.key(seed), 8)
    part_splits = jax.random.split(jax.random.fold_in(key_of[7], part), 8)
    inputs = noise(part_splits[0], (TOKENS, MODEL_WIDTH), 1.0, 6.0, ((0, 16),))
    output_gradient = noise(part_splits[1], (TOKENS, KEY_WIDTH), 1.0, 6.0, ((0, 16),))
    token_adapter_index_keys = jax.random.split(jax.random.fold_in(part_splits[2], 1), TOKENS // TOK_DEV)
    token_adapter_index_turns = jax.random.permutation(jax.random.fold_in(part_splits[2], 3), TOKENS // TOK_DEV)
    token_adapter_index = jax.vmap(lambda own, number: deal_out(jax.random.fold_in(part_splits[2], 2), own, number, TOK_DEV, ADAPTER_TOTAL, 1, CAP, 2))(token_adapter_index_keys, token_adapter_index_turns).reshape((TOKENS, 1))
    owner_index_map = jax.random.permutation(key_of[3], ADAPTER_TOTAL).astype(jnp.int32)
    frozen_key_weight = noise(key_of[4], (MODEL_WIDTH, KEY_WIDTH), MODEL_WIDTH ** -0.5, 0.0625, ((0, 16),))
    down_panels = noise(key_of[5], (ADAPTER_TOTAL, MODEL_WIDTH, ADAPTER_RANK), MODEL_WIDTH ** -0.5, 0.0625, ((0, 16),))
    up_panels = noise(key_of[6], (ADAPTER_TOTAL, ADAPTER_RANK, KEY_WIDTH), KEY_WIDTH ** -0.5, 0.1875, ((0, 16),))
    return {"inputs": inputs, "output_gradient": output_gradient, "token_adapter_index": token_adapter_index, "owner_index_map": owner_index_map, "frozen_key_weight": frozen_key_weight, "down_panels": down_panels, "up_panels": up_panels}


adapter_scale = 2.0


def reference(inputs, output_gradient, token_adapter_index, owner_index_map, frozen_key_weight, down_panels, up_panels):
    adapter_index = token_adapter_index[:, 0].astype(jnp.int32)
    adapter_list = owner_index_map.shape[0]
    width = N_DP * CAP
    order = jnp.argsort(adapter_index, stable=True).astype(jnp.int32)
    counts = jnp.sum((adapter_index[:, None] == jnp.arange(adapter_list, dtype=jnp.int32)[None, :]).astype(jnp.int32), axis=0)
    starts = (jnp.cumsum(counts) - counts).astype(jnp.int32)

    def adapter_rows(adapter_slot):
        offsets = jnp.arange(width, dtype=jnp.int32)
        valid = offsets < counts[adapter_slot]
        index = order[jnp.clip(starts[adapter_slot] + offsets, 0, adapter_index.shape[0] - 1)]
        input_rows = jnp.where(valid[:, None], inputs[index], jnp.zeros((), inputs.dtype))
        gradient_rows = jnp.where(valid[:, None], output_gradient[index], jnp.zeros((), output_gradient.dtype))
        down_panel = down_panels[owner_index_map[adapter_slot]]
        up_panel = up_panels[owner_index_map[adapter_slot]]
        hidden_state = jnp.dot(input_rows, down_panel, preferred_element_type=jnp.float32).astype(jnp.bfloat16)
        up_gradient_local = adapter_scale * jnp.dot(hidden_state.T, gradient_rows, preferred_element_type=jnp.float32)
        adapter_gradient = (adapter_scale * jnp.dot(gradient_rows, up_panel.T, preferred_element_type=jnp.float32)).astype(jnp.bfloat16)
        down_gradient_local = jnp.dot(input_rows.T, adapter_gradient, preferred_element_type=jnp.float32)
        adapter_input = jnp.dot(adapter_gradient, down_panel.T, preferred_element_type=jnp.float32).astype(jnp.bfloat16)
        return down_gradient_local, up_gradient_local, adapter_input

    down_gradient_local, up_gradient_local, adapter_input = lax.map(adapter_rows, jnp.arange(adapter_list, dtype=jnp.int32))
    inverse = jnp.argsort(order, stable=True).astype(jnp.int32)
    within_index = inverse - starts[adapter_index]
    adapter_tokens = adapter_input[adapter_index, within_index].astype(jnp.float32)
    base_term = jnp.dot(output_gradient, frozen_key_weight.T, preferred_element_type=jnp.float32)
    input_gradient = (base_term + adapter_tokens).astype(jnp.bfloat16)
    owned = jnp.argsort(owner_index_map, stable=True).astype(jnp.int32)
    return input_gradient, down_gradient_local[owned], up_gradient_local[owned]
```

```python
import functools

import jax
import jax.numpy as jnp
from jax import lax
from jax.experimental import pallas as pl
from jax.experimental.pallas import tpu as pltpu
from jax.sharding import PartitionSpec as P

adapter_scale = 2.0
MESH = pl.DeviceIdType.MESH
ROWS = 16


def exchange_kernel(
    G,
    S,
    N,
    rank,
    x_ref,
    dyr_ref,
    dy_ref,
    w_ref,
    pt_ref,
    place_ref,
    hot_ref,
    q_ref,
    out_ref,
    rx_ref,
    rdy_out,
    lg_out,
    rdy,
    lg,
    rlg,
    wsh,
    psh,
    dyp,
    tiles,
    osend,
    expand,
    local_sem,
    dy_s,
    dy_r,
    lg_s,
    lg_r,
    p_s,
    p_r,
    x_s,
    x_r,
    w_s,
    w_r,
    b_s,
    b_r,
    t_s,
    t_r,
    o_s,
    o_r,
):
    PL = G * S
    L = N // S
    RG = w_ref.shape[0] // G
    T = dy_ref.shape[0]
    me_g = lax.axis_index("groups")
    me = lax.axis_index("dp")
    me_z = me // S
    me_s = lax.rem(me, S)
    me_p = me_g * S + me_s

    def group_dev(k):
        return lax.rem(me + k, N)

    def group_src(k):
        return lax.rem(me + N - k, N)

    def plane_dev(k):
        p = lax.rem(me_p + k, PL)
        return (p // S, me_z * S + lax.rem(p, S)), p

    def line_dev(k):
        return (me_g, lax.rem(me_z + k, L) * S + me_s)

    def rcopy(src, dst, ss, rs, dev):
        return pltpu.make_async_remote_copy(
            src_ref=src, dst_ref=dst, send_sem=ss, recv_sem=rs, device_id=dev, device_id_type=MESH
        )

    def each(lo, hi, body):
        def step(k, c):
            body(k)
            return c

        lax.fori_loop(lo, hi, step, 0)

    barrier = pltpu.get_barrier_semaphore()
    each(
        1,
        N,
        lambda k: pl.semaphore_signal(
            barrier, inc=1, device_id=(me_g, group_dev(k)), device_id_type=MESH
        ),
    )
    others = (G - 1) * S

    def greet(k):
        gg = lax.rem(me_g + 1 + k // S, G)
        pl.semaphore_signal(
            barrier,
            inc=1,
            device_id=(gg, me_z * S + lax.rem(k, S)),
            device_id_type=MESH,
        )

    each(0, others, greet)
    pl.semaphore_wait(barrier, N - 1 + others)

    def dy_copy(k):
        d = group_dev(k)
        return rcopy(dyr_ref.at[d], rdy.at[me], dy_s.at[k], dy_r.at[k], (me_g, d))

    each(1, N, lambda k: dy_copy(k).start())
    own_dy = pltpu.make_async_copy(dyr_ref.at[me], rdy.at[me], local_sem.at[0])
    own_dy.start()

    def b_copy(k):
        dev, _ = plane_dev(k)
        return rcopy(dy_ref, dyp.at[me_p], b_s.at[k], b_r.at[k], dev)

    each(1, PL, lambda k: b_copy(k).start())
    own_b = pltpu.make_async_copy(dy_ref, dyp.at[me_p], local_sem.at[1])
    own_b.start()

    w_part = w_ref.at[pl.ds(pl.multiple_of(me_g * RG, RG), RG)]

    def w_copy(k):
        return rcopy(w_part, wsh.at[me_z], w_s.at[k], w_r.at[k], line_dev(k))

    each(1, L, lambda k: w_copy(k).start())
    own_w = pltpu.make_async_copy(w_part, wsh.at[me_z], local_sem.at[2])
    own_w.start()

    def p_copy(k):
        d = group_dev(k)
        return rcopy(pt_ref.at[lax.rem(d, S)], psh.at[me], p_s.at[k], p_r.at[k], (me_g, d))

    each(1, N, lambda k: p_copy(k).start())
    own_p = pltpu.make_async_copy(pt_ref.at[me_s], psh.at[me], local_sem.at[3])
    own_p.start()

    each(1, N, lambda k: dy_copy(k).wait_recv())
    own_dy.wait()
    value = adapter_scale * lax.dot_general(
        rdy[...].reshape(N * ROWS, rdy.shape[2]),
        q_ref[...],
        (((1,), (1,)), ((), ())),
        preferred_element_type=jnp.float32,
    )
    lg[...] = value.astype(jnp.bfloat16).reshape(lg.shape)

    def lg_copy(k):
        d = group_dev(k)
        return rcopy(lg.at[d], rlg.at[me], lg_s.at[k], lg_r.at[k], (me_g, d))

    each(1, N, lambda k: lg_copy(k).start())
    own_lg = pltpu.make_async_copy(lg.at[me], rlg.at[me], local_sem.at[4])
    own_lg.start()
    save_dy = pltpu.make_async_copy(rdy, rdy_out, local_sem.at[5])
    save_dy.start()
    save_lg = pltpu.make_async_copy(lg, lg_out, local_sem.at[6])
    save_lg.start()

    def x_copy(k):
        d = group_dev(k)
        return rcopy(x_ref.at[d], rx_ref.at[me], x_s.at[k], x_r.at[k], (me_g, d))

    each(1, N, lambda k: x_copy(k).start())
    own_x = pltpu.make_async_copy(x_ref.at[me], rx_ref.at[me], local_sem.at[7])
    own_x.start()

    TL = tiles.shape[2]
    row = lax.broadcasted_iota(jnp.int32, (TL, N * rank), 0)
    col = lax.broadcasted_iota(jnp.int32, (TL, N * rank), 1)
    expand[0] = jnp.where(row == lax.rem(col, rank), 1.0, 0.0).astype(jnp.bfloat16)
    expand[1] = jnp.where(row - rank == col // rank, 1.0, 0.0).astype(jnp.bfloat16)

    each(1, N, lambda k: lg_copy(k).wait_recv())
    own_lg.wait()
    tokens = jnp.dot(
        place_ref[...], rlg[...].reshape(N * ROWS, TL), preferred_element_type=jnp.float32
    )
    tiles[me_p] = tokens.astype(jnp.bfloat16) + hot_ref[...]

    def t_copy(k):
        dev, _ = plane_dev(k)
        return rcopy(tiles.at[me_p], tiles.at[me_p], t_s.at[k], t_r.at[k], dev)

    each(1, PL, lambda k: t_copy(k).start())
    each(1, PL, lambda k: b_copy(k).wait_recv())
    own_b.wait()
    each(1, L, lambda k: w_copy(k).wait_recv())
    own_w.wait()
    each(1, PL, lambda k: t_copy(k).wait_recv())
    each(1, N, lambda k: p_copy(k).wait_recv())
    own_p.wait()

    def o_copy(k):
        dev, p = plane_dev(k)
        return rcopy(osend.at[p], out_ref.at[me_p], o_s.at[k], o_r.at[k], dev)

    def block(k):
        p = lax.rem(me_p + k, PL)
        base = lax.dot_general(
            dyp[p],
            wsh[...].reshape(L * RG, wsh.shape[2]),
            (((1,), (1,)), ((), ())),
            preferred_element_type=jnp.float32,
        )
        tile = tiles[p]
        spread = jnp.dot(tile, expand[0], preferred_element_type=jnp.float32)
        chosen = jnp.dot(tile, expand[1], preferred_element_type=jnp.float32)
        masked = (spread * chosen).astype(jnp.bfloat16)
        term = jnp.dot(
            masked, psh[...].reshape(N * rank, psh.shape[2]), preferred_element_type=jnp.float32
        ).astype(jnp.bfloat16)
        osend[p] = (base + term.astype(jnp.float32)).astype(jnp.bfloat16)

    def block_and_send(k):
        block(k)
        o_copy(k).start()

    each(1, PL, block_and_send)
    block(0)
    own_o = pltpu.make_async_copy(osend.at[me_p], out_ref.at[me_p], local_sem.at[8])
    own_o.start()

    each(1, PL, lambda k: o_copy(k).wait_recv())
    each(1, N, lambda k: x_copy(k).wait_recv())
    own_x.wait()
    own_o.wait()
    save_dy.wait()
    save_lg.wait()
    each(1, N, lambda k: dy_copy(k).wait_send())
    each(1, N, lambda k: lg_copy(k).wait_send())
    each(1, N, lambda k: p_copy(k).wait_send())
    each(1, N, lambda k: x_copy(k).wait_send())
    each(1, L, lambda k: w_copy(k).wait_send())
    each(1, PL, lambda k: b_copy(k).wait_send())
    each(1, PL, lambda k: t_copy(k).wait_send())
    each(1, PL, lambda k: o_copy(k).wait_send())


def per_device(
    G,
    inputs,
    output_gradient,
    token_adapter_index,
    owner_index_map,
    frozen_key_weight,
    down_panels,
    up_panels,
):
    N = lax.axis_size("dp")
    S = max(1, 8 // G)
    L = N // S
    PL = G * S
    T, D = inputs.shape
    K = output_gradient.shape[1]
    R = frozen_key_weight.shape[0]
    RG = R // G
    rank = down_panels.shape[2]
    cap = max(2, 3 * T // (2 * N))
    TL = -(-(rank + N) // 128) * 128
    bf16 = jnp.bfloat16

    index = token_adapter_index[:, 0]
    hot = index[:, None] == jnp.arange(N, dtype=jnp.int32)[None, :]
    before = jnp.arange(T)[:, None] > jnp.arange(T)[None, :]
    earlier = jnp.dot(before.astype(bf16), hot.astype(bf16), preferred_element_type=jnp.float32)
    place_in = jnp.sum(jnp.where(hot, earlier, 0.0), axis=1).astype(jnp.int32)
    owner = jnp.sum(jnp.where(hot, owner_index_map[None, :], 0), axis=1)
    slots12 = (jnp.arange(N * cap, dtype=jnp.int32)[:, None] == (owner * cap + place_in)[None, :])
    slots16 = (jnp.arange(N * ROWS, dtype=jnp.int32)[:, None] == (owner * ROWS + place_in)[None, :])
    place_x = slots12.astype(bf16)
    place_dy = slots16.astype(bf16)
    place_t = (
        (owner * ROWS + place_in)[:, None] == jnp.arange(N * ROWS, dtype=jnp.int32)[None, :]
    ).astype(bf16)
    owner_hot = (owner[:, None] == jnp.arange(TL, dtype=jnp.int32)[None, :] - rank).astype(bf16)

    send_x = jnp.dot(place_x, inputs, preferred_element_type=jnp.float32).astype(bf16)
    send_x = send_x.reshape(N, cap * D // 512, 512)
    send_dy = jnp.dot(place_dy, output_gradient, preferred_element_type=jnp.float32).astype(bf16)
    send_dy = send_dy.reshape(N, ROWS, K)

    panel = down_panels[0]
    group = lax.axis_index("groups")
    mine = lax.dynamic_index_in_dim(panel.reshape(L, S, G, RG, rank), group, 2, keepdims=False)
    shares = mine.transpose(1, 3, 0, 2).reshape(S, rank, L * RG)
    up_panel = up_panels[0]
    up_padded = jnp.pad(up_panel, ((0, TL - rank), (0, 0)))

    anyspace = pl.BlockSpec(memory_space=pl.ANY)
    vmem = pl.BlockSpec(memory_space=pltpu.VMEM)
    dma = pltpu.SemaphoreType.DMA
    outs, rx, rdy, lg = pl.pallas_call(
        functools.partial(exchange_kernel, G, S, N, rank),
        out_shape=(
            jax.ShapeDtypeStruct((PL, T, L * RG), bf16),
            jax.ShapeDtypeStruct(send_x.shape, bf16),
            jax.ShapeDtypeStruct(send_dy.shape, bf16),
            jax.ShapeDtypeStruct((N, ROWS, TL), bf16),
        ),
        in_specs=[anyspace] * 5 + [vmem] * 3,
        out_specs=[anyspace] * 4,
        scratch_shapes=[
            pltpu.VMEM((N, ROWS, K), bf16),
            pltpu.VMEM((N, ROWS, TL), bf16),
            pltpu.VMEM((N, ROWS, TL), bf16),
            pltpu.VMEM((L, RG, K), bf16),
            pltpu.VMEM((N, rank, L * RG), bf16),
            pltpu.VMEM((PL, T, K), bf16),
            pltpu.VMEM((PL, T, TL), bf16),
            pltpu.VMEM((PL, T, L * RG), bf16),
            pltpu.VMEM((2, TL, N * rank), bf16),
            dma((9,)),
        ]
        + [dma((N,))] * 8
        + [dma((L,))] * 2
        + [dma((PL,))] * 6,
        compiler_params=pltpu.CompilerParams(
            collective_id=0, has_side_effects=True, vmem_limit_bytes=48 * 1024 * 1024
        ),
        cost_estimate=pl.CostEstimate(
            flops=4 * PL * T * L * RG * K, bytes_accessed=16 * 1024 * 1024, transcendentals=0
        ),
        name="exchange",
    )(send_x, send_dy, output_gradient, frozen_key_weight, shares, place_t, owner_hot, up_padded)

    input_gradient = (
        outs.reshape(G, S, T, L, RG).transpose(2, 3, 1, 0, 4).reshape(T, D)
    )
    rows = rx.reshape(N * cap, D)
    gradient_rows = rdy[:, :cap].reshape(N * cap, K)
    lora = lg[:, :cap, :rank].reshape(N * cap, rank)
    contract_rows = (((0,), (0,)), ((), ()))
    hidden = jnp.dot(rows, panel, preferred_element_type=jnp.float32).astype(bf16)
    up_gradient = adapter_scale * lax.dot_general(
        hidden, gradient_rows, contract_rows, preferred_element_type=jnp.float32
    )
    down_gradient = lax.dot_general(
        rows, lora, contract_rows, preferred_element_type=jnp.float32
    )
    return (input_gradient, down_gradient[None], up_gradient[None])


def solution(mesh):
    in_specs = (
        P(("groups", "dp"), None),
        P(("groups", "dp"), None),
        P(("groups", "dp"), None),
        P(),
        P("dp", None),
        P("dp", None, None),
        P("dp", None, None),
    )
    out_specs = (
        P(("groups", "dp"), None),
        P(("groups", "dp"), None, None),
        P(("groups", "dp"), None, None),
    )
    return jax.shard_map(
        functools.partial(per_device, mesh.shape["groups"]),
        mesh=mesh,
        in_specs=in_specs,
        out_specs=out_specs,
        check_vma=False,
    )
```

```python
import functools

import jax
import jax.numpy as jnp
from jax import lax
from jax.experimental import pallas as pl
from jax.experimental.pallas import tpu as pltpu
from jax.sharding import PartitionSpec as P

adapter_scale = 2.0
MESH = pl.DeviceIdType.MESH
ROWS = 16
CHUNKS = 4
NT = (((1,), (1,)), ((), ()))
TN = (((0,), (0,)), ((), ()))


def ceil16(n):
    return -(-n // 16) * 16


def each(lo, hi, body):
    def step(k, c):
        body(k)
        return c

    lax.fori_loop(lo, hi, step, 0)


def exchange_kernel(
    G,
    S,
    N,
    cap,
    x_ref,
    dy_ref,
    w_ref,
    pt_ref,
    share_ref,
    place_x_ref,
    place_dy_ref,
    place_ref,
    hot_ref,
    q_ref,
    out_ref,
    down_ref,
    up_ref,
    dyr,
    rdy,
    lg,
    rlg,
    wsh,
    psh,
    share,
    dyp,
    tiles,
    osend,
    expand,
    xs,
    mid,
    hs,
    rows,
    hid,
    local_sem,
    dy_s,
    dy_r,
    lg_s,
    lg_r,
    wr_s,
    wl_s,
    w_r,
    pr_s,
    pl_s,
    p_r,
    pp_s,
    pp_r,
    h1_s,
    h1_r,
    h2_s,
    h2_r,
    b_s,
    b_r,
    t_s,
    t_r,
    o_s,
    o_r,
):
    bf16 = jnp.bfloat16
    f32 = jnp.float32
    PL = G * S
    L = N // S
    R = w_ref.shape[0]
    RG = R // G
    K = dy_ref.shape[1]
    rank = pt_ref.shape[0]
    C, _, RP, CD = xs.shape
    RQ = rows.shape[2]
    TL = tiles.shape[2]
    aligned = RG % 128 == 0
    pieces = L if aligned else 1
    me_g = lax.axis_index("groups")
    me = lax.axis_index("dp")
    me_z = me // S
    me_s = lax.rem(me, S)
    me_p = me_g * S + me_s

    def group_dev(k):
        return lax.rem(me + k, N)

    def plane_dev(k):
        p = lax.rem(me_p + k, PL)
        return (p // S, me_z * S + lax.rem(p, S)), p

    def line_dev(z):
        return (me_g, z * S + me_s)

    def rcopy(src, dst, ss, rs, dev):
        return pltpu.make_async_remote_copy(
            src_ref=src, dst_ref=dst, send_sem=ss, recv_sem=rs, device_id=dev, device_id_type=MESH
        )

    barrier = pltpu.get_barrier_semaphore()
    each(
        1,
        N,
        lambda k: pl.semaphore_signal(
            barrier, inc=1, device_id=(me_g, group_dev(k)), device_id_type=MESH
        ),
    )
    others = (G - 1) * S

    def greet(k):
        gg = lax.rem(me_g + 1 + k // S, G)
        pl.semaphore_signal(
            barrier, inc=1, device_id=(gg, me_z * S + lax.rem(k, S)), device_id_type=MESH
        )

    each(0, others, greet)
    dyr[...] = (
        jnp.dot(place_dy_ref[...], dy_ref[...], preferred_element_type=f32)
        .astype(bf16)
        .reshape(dyr.shape)
    )
    if aligned:
        for s in range(S):
            for z in range(L):
                start = pl.multiple_of((z * S + s) * R + me_g * RG, 128)
                share[s, :, z * RG : (z + 1) * RG] = pt_ref[:, pl.ds(start, RG)]
    else:
        share[...] = share_ref[...]
    pl.semaphore_wait(barrier, N - 1 + others)

    def dy_copy(k):
        d = group_dev(k)
        return rcopy(dyr.at[d], rdy.at[me], dy_s.at[k], dy_r.at[k], (me_g, d))

    each(1, N, lambda k: dy_copy(k).start())
    own_dy = pltpu.make_async_copy(dyr.at[me], rdy.at[me], local_sem.at[0])
    own_dy.start()

    w_part = w_ref.at[pl.ds(pl.multiple_of(me_g * RG, RG), RG)]
    own_w = pltpu.make_async_copy(w_part, wsh.at[me_z], local_sem.at[2])
    own_w.start()

    def pp_copy(k):
        s = lax.rem(me_s + k, S)
        return rcopy(
            share.at[s], psh.at[me_z, me_s], pp_s.at[k], pp_r.at[k], (me_g, me_z * S + s)
        )

    each(1, S, lambda k: pp_copy(k).start())
    own_p = pltpu.make_async_copy(share.at[me_s], psh.at[me_z, me_s], local_sem.at[3])
    own_p.start()

    def line_copies(buf, right_s, left_s, recv):
        def right(b):
            return rcopy(buf.at[b], buf.at[b], right_s.at[b], recv.at[b], line_dev(me_z + 1))

        def left(b):
            return rcopy(buf.at[b], buf.at[b], left_s.at[b], recv.at[b], line_dev(me_z - 1))

        return right, left

    def line_begin(right, left):
        @pl.when(me_z < L - 1)
        def _():
            right(me_z).start()

        @pl.when(me_z > 0)
        def _():
            left(me_z).start()

    def line_step(right, left, t):
        @pl.when(me_z - t >= 0)
        def _():
            right(me_z - t).wait_recv()

            @pl.when(me_z < L - 1)
            def _():
                right(me_z - t).start()

        @pl.when(me_z + t < L)
        def _():
            left(me_z + t).wait_recv()

            @pl.when(me_z > 0)
            def _():
                left(me_z + t).start()

    def line_end(right, left):
        def one(b):
            @pl.when(jnp.logical_and(b <= me_z, me_z < L - 1))
            def _():
                right(b).wait_send()

            @pl.when(jnp.logical_and(b >= me_z, me_z > 0))
            def _():
                left(b).wait_send()

        each(0, L, one)

    w_line = line_copies(wsh, wr_s, wl_s, w_r)
    p_line = line_copies(psh, pr_s, pl_s, p_r)

    def h1_copy(c, k):
        z = lax.rem(me_z + k, L)
        i = c * L + k
        return rcopy(xs.at[c, z], mid.at[c, me_z], h1_s.at[i], h1_r.at[i], line_dev(z))

    def own_mid(c):
        return pltpu.make_async_copy(xs.at[c, me_z], mid.at[c, me_z], local_sem.at[16 + c])

    def send_rows(c):
        start = pl.multiple_of(c * CD, CD)
        xs[c] = (
            jnp.dot(place_x_ref[...], x_ref[:, pl.ds(start, CD)], preferred_element_type=f32)
            .astype(bf16)
            .reshape(L, RP, CD)
        )
        each(1, L, lambda k: h1_copy(c, k).start())
        own_mid(c).start()

    def h2_copy(c, k):
        s = lax.rem(me_s + k, S)
        i = c * S + k
        return rcopy(
            hs.at[c, s], rows.at[c, me_s], h2_s.at[i], h2_r.at[i], (me_g, me_z * S + s)
        )

    def regroup(c):
        each(1, L, lambda k: h1_copy(c, k).wait_recv())
        own_mid(c).wait()

        def pick(s):
            q = lax.broadcasted_iota(jnp.int32, (RQ, L * RP), 0)
            j = lax.broadcasted_iota(jnp.int32, (RQ, L * RP), 1)
            hit = (j == (q // cap) * RP + s * cap + lax.rem(q, cap)) & (q < L * cap)
            sel = jnp.where(hit, 1.0, 0.0).astype(bf16)
            return jnp.dot(
                sel, mid[c].reshape(L * RP, CD), preferred_element_type=f32
            ).astype(bf16)

        def part(k):
            s = lax.rem(me_s + k, S)
            hs[c, s] = pick(s)
            h2_copy(c, k).start()

        each(1, S, part)
        rows[c, me_s] = pick(me_s)

    own_w.wait()
    line_begin(*w_line)
    send_rows(0)
    each(1, S, lambda k: pp_copy(k).wait_recv())
    own_p.wait()
    line_begin(*p_line)
    each(1, C, send_rows)

    def b_copy(k):
        dev, _ = plane_dev(k)
        return rcopy(dy_ref, dyp.at[me_p], b_s.at[k], b_r.at[k], dev)

    each(1, PL, lambda k: b_copy(k).start())
    own_b = pltpu.make_async_copy(dy_ref, dyp.at[me_p], local_sem.at[1])
    own_b.start()

    each(1, N, lambda k: dy_copy(k).wait_recv())
    own_dy.wait()
    value = adapter_scale * lax.dot_general(
        rdy[...].reshape(N * ROWS, K), q_ref[...], NT, preferred_element_type=f32
    )
    lg[...] = value.astype(bf16).reshape(lg.shape)

    def lg_copy(k):
        d = group_dev(k)
        return rcopy(lg.at[d], rlg.at[me], lg_s.at[k], lg_r.at[k], (me_g, d))

    each(1, N, lambda k: lg_copy(k).start())
    own_lg = pltpu.make_async_copy(lg.at[me], rlg.at[me], local_sem.at[4])
    own_lg.start()
    each(1, L, lambda t: line_step(*w_line, t))

    row = lax.broadcasted_iota(jnp.int32, (TL, N * rank), 0)
    col = lax.broadcasted_iota(jnp.int32, (TL, N * rank), 1)
    expand[0] = jnp.where(row == lax.rem(col, rank), 1.0, 0.0).astype(bf16)
    expand[1] = jnp.where(row - rank == col // rank, 1.0, 0.0).astype(bf16)

    each(1, N, lambda k: lg_copy(k).wait_recv())
    own_lg.wait()
    tokens = jnp.dot(
        place_ref[...], rlg[...].reshape(N * ROWS, TL), preferred_element_type=f32
    )
    tiles[me_p] = tokens.astype(bf16) + hot_ref[...]

    def t_copy(k):
        dev, _ = plane_dev(k)
        return rcopy(tiles.at[me_p], tiles.at[me_p], t_s.at[k], t_r.at[k], dev)

    each(1, PL, lambda k: t_copy(k).start())

    each(1, L, lambda t: line_step(*p_line, t))
    regroup(0)
    each(1, PL, lambda k: b_copy(k).wait_recv())
    own_b.wait()
    each(1, PL, lambda k: t_copy(k).wait_recv())

    def o_copy(k, i):
        dev, p = plane_dev(k)
        if not aligned:
            return rcopy(osend.at[p], out_ref.at[me_p], o_s.at[k], o_r.at[k], dev)
        start = pl.multiple_of((i * S + me_s) * R + me_g * RG, 128)
        return rcopy(
            osend.at[p, :, pl.ds(i * RG, RG)],
            out_ref.at[:, pl.ds(start, RG)],
            o_s.at[k * L + i],
            o_r.at[k * L + i],
            dev,
        )

    def own_out(i):
        if not aligned:
            return pltpu.make_async_copy(osend.at[me_p], out_ref.at[me_p], local_sem.at[8])
        start = pl.multiple_of((i * S + me_s) * R + me_g * RG, 128)
        return pltpu.make_async_copy(
            osend.at[me_p, :, pl.ds(i * RG, RG)],
            out_ref.at[:, pl.ds(start, RG)],
            local_sem.at[8 + i],
        )

    def block(k):
        p = lax.rem(me_p + k, PL)
        base = lax.dot_general(
            dyp[p], wsh[...].reshape(L * RG, K), NT, preferred_element_type=f32
        )
        tile = tiles[p]
        spread = jnp.dot(tile, expand[0], preferred_element_type=f32)
        chosen = jnp.dot(tile, expand[1], preferred_element_type=f32)
        masked = (spread * chosen).astype(bf16)
        term = jnp.dot(
            masked, psh[...].reshape(N * rank, L * RG), preferred_element_type=f32
        ).astype(bf16)
        osend[p] = (base + term.astype(f32)).astype(bf16)

    def block_and_send(k):
        block(k)
        for i in range(pieces):
            o_copy(k, i).start()

    each(1, PL, block_and_send)
    each(1, C, regroup)
    block(0)
    for i in range(pieces):
        own_out(i).start()

    q = lax.broadcasted_iota(jnp.int32, (S * RQ, N * ROWS), 0)
    j = lax.broadcasted_iota(jnp.int32, (S * RQ, N * ROWS), 1)
    inside = lax.rem(q, RQ)
    slot = ((inside // cap) * S + q // RQ) * ROWS + lax.rem(inside, cap)
    sel = jnp.where((j == slot) & (inside < L * cap), 1.0, 0.0).astype(bf16)
    lora = jnp.dot(sel, lg[...].reshape(N * ROWS, TL), preferred_element_type=f32).astype(bf16)
    grad = jnp.dot(sel, rdy[...].reshape(N * ROWS, K), preferred_element_type=f32).astype(bf16)

    hid[...] = jnp.zeros_like(hid)

    def finish(c):
        each(1, S, lambda k: h2_copy(c, k).wait_recv())
        start = pl.multiple_of(c * CD, CD)
        rc = rows[c].reshape(S * RQ, CD)
        hid[...] += lax.dot_general(
            rc, pt_ref[:, pl.ds(start, CD)], NT, preferred_element_type=f32
        )
        down_ref[:, pl.ds(start, CD)] = lax.dot_general(
            lora, rc, TN, preferred_element_type=f32
        )[:rank]

    each(0, C, finish)
    up_ref[...] = adapter_scale * lax.dot_general(
        hid[...].astype(bf16), grad, TN, preferred_element_type=f32
    )

    for i in range(pieces):
        each(1, PL, lambda k: o_copy(k, i).wait_recv())
        own_out(i).wait()
    each(1, N, lambda k: dy_copy(k).wait_send())
    each(1, N, lambda k: lg_copy(k).wait_send())
    each(1, S, lambda k: pp_copy(k).wait_send())
    for c in range(C):
        each(1, L, lambda k: h1_copy(c, k).wait_send())
        each(1, S, lambda k: h2_copy(c, k).wait_send())
    line_end(*w_line)
    line_end(*p_line)
    each(1, PL, lambda k: b_copy(k).wait_send())
    each(1, PL, lambda k: t_copy(k).wait_send())
    for i in range(pieces):
        each(1, PL, lambda k: o_copy(k, i).wait_send())


def per_device(
    G,
    inputs,
    output_gradient,
    token_adapter_index,
    owner_index_map,
    frozen_key_weight,
    down_panels,
    up_panels,
):
    N = lax.axis_size("dp")
    S = max(1, 8 // G)
    L = N // S
    PL = G * S
    T, D = inputs.shape
    K = output_gradient.shape[1]
    R = frozen_key_weight.shape[0]
    RG = R // G
    rank = down_panels.shape[2]
    cap = max(2, 3 * T // (2 * N))
    TL = -(-(rank + N) // 128) * 128
    RP = ceil16(S * cap)
    RQ = ceil16(L * cap)
    C = CHUNKS
    CD = D // C
    aligned = RG % 128 == 0
    pieces = L if aligned else 1
    bf16 = jnp.bfloat16
    f32 = jnp.float32

    index = token_adapter_index[:, 0]
    hot = index[:, None] == jnp.arange(N, dtype=jnp.int32)[None, :]
    before = jnp.arange(T)[:, None] > jnp.arange(T)[None, :]
    earlier = jnp.dot(before.astype(bf16), hot.astype(bf16), preferred_element_type=f32)
    turn = jnp.sum(jnp.where(hot, earlier, 0.0), axis=1).astype(jnp.int32)
    owner = jnp.sum(jnp.where(hot, owner_index_map[None, :], 0), axis=1)

    def numbers(n):
        return jnp.arange(n, dtype=jnp.int32)

    x_slot = (owner // S) * RP + (owner % S) * cap + turn
    place_x = (numbers(L * RP)[:, None] == x_slot[None, :]).astype(bf16)
    slot = owner * ROWS + turn
    place_dy = (numbers(N * ROWS)[:, None] == slot[None, :]).astype(bf16)
    place_t = (slot[:, None] == numbers(N * ROWS)[None, :]).astype(bf16)
    owner_hot = (owner[:, None] == numbers(TL)[None, :] - rank).astype(bf16)

    turned = down_panels[0].T
    if aligned:
        shares = turned
    else:
        group = lax.axis_index("groups")
        mine = lax.dynamic_index_in_dim(
            turned.reshape(rank, L, S, G, RG), group, 3, keepdims=False
        )
        shares = mine.transpose(2, 0, 1, 3).reshape(S, rank, L * RG)
    up_padded = jnp.pad(up_panels[0], ((0, TL - rank), (0, 0)))

    anyspace = pl.BlockSpec(memory_space=pl.ANY)
    vmem = pl.BlockSpec(memory_space=pltpu.VMEM)
    dma = pltpu.SemaphoreType.DMA
    out_shape = (T, D) if aligned else (PL, T, L * RG)
    outs, down, up = pl.pallas_call(
        functools.partial(exchange_kernel, G, S, N, cap),
        out_shape=(
            jax.ShapeDtypeStruct(out_shape, bf16),
            jax.ShapeDtypeStruct((rank, D), f32),
            jax.ShapeDtypeStruct((rank, K), f32),
        ),
        in_specs=[
            vmem,
            vmem,
            anyspace,
            vmem,
            anyspace if aligned else vmem,
            vmem,
            vmem,
            vmem,
            vmem,
            vmem,
        ],
        out_specs=[anyspace, vmem, vmem],
        scratch_shapes=[
            pltpu.VMEM((N, ROWS, K), bf16),
            pltpu.VMEM((N, ROWS, K), bf16),
            pltpu.VMEM((N, ROWS, TL), bf16),
            pltpu.VMEM((N, ROWS, TL), bf16),
            pltpu.VMEM((L, RG, K), bf16),
            pltpu.VMEM((L, S, rank, L * RG), bf16),
            pltpu.VMEM((S, rank, L * RG), bf16),
            pltpu.VMEM((PL, T, K), bf16),
            pltpu.VMEM((PL, T, TL), bf16),
            pltpu.VMEM((PL, T, L * RG), bf16),
            pltpu.VMEM((2, TL, N * rank), bf16),
            pltpu.VMEM((C, L, RP, CD), bf16),
            pltpu.VMEM((C, L, RP, CD), bf16),
            pltpu.VMEM((C, S, RQ, CD), bf16),
            pltpu.VMEM((C, S, RQ, CD), bf16),
            pltpu.VMEM((S * RQ, rank), f32),
            dma((16 + C,)),
        ]
        + [dma((N,))] * 4
        + [dma((L,))] * 6
        + [dma((S,))] * 2
        + [dma((C * L,))] * 2
        + [dma((C * S,))] * 2
        + [dma((PL,))] * 4
        + [dma((PL * pieces,))] * 2,
        compiler_params=pltpu.CompilerParams(
            collective_id=0, has_side_effects=True, vmem_limit_bytes=56 * 1024 * 1024
        ),
        cost_estimate=pl.CostEstimate(
            flops=4 * PL * T * L * RG * K, bytes_accessed=16 * 1024 * 1024, transcendentals=0
        ),
        name="exchange",
    )(
        inputs,
        output_gradient,
        frozen_key_weight,
        turned,
        shares,
        place_x,
        place_dy,
        place_t,
        owner_hot,
        up_padded,
    )

    if not aligned:
        outs = outs.reshape(G, S, T, L, RG).transpose(2, 3, 1, 0, 4).reshape(T, D)
    return (outs, down.T[None], up[None])


def solution(mesh):
    in_specs = (
        P(("groups", "dp"), None),
        P(("groups", "dp"), None),
        P(("groups", "dp"), None),
        P(),
        P("dp", None),
        P("dp", None, None),
        P("dp", None, None),
    )
    out_specs = (
        P(("groups", "dp"), None),
        P(("groups", "dp"), None, None),
        P(("groups", "dp"), None, None),
    )
    return jax.shard_map(
        functools.partial(per_device, mesh.shape["groups"]),
        mesh=mesh,
        in_specs=in_specs,
        out_specs=out_specs,
        check_vma=False,
    )
```

```python
import functools

import jax
import jax.numpy as jnp
from jax import lax
from jax.experimental import pallas as pl
from jax.experimental.pallas import tpu as pltpu
from jax.sharding import PartitionSpec as P

adapter_scale = 2.0
MESH = pl.DeviceIdType.MESH
ROWS = 16
CHUNKS = 4
NT = (((1,), (1,)), ((), ()))
TN = (((0,), (0,)), ((), ()))


def ceil16(n):
    return -(-n // 16) * 16


def each(lo, hi, body):
    def step(k, c):
        body(k)
        return c

    lax.fori_loop(lo, hi, step, 0)


def exchange_kernel(
    G,
    S,
    N,
    cap,
    x_ref,
    dy_ref,
    w_ref,
    pt_ref,
    share_ref,
    place_x_ref,
    place_dy_ref,
    place_ref,
    hot_ref,
    q_ref,
    out_ref,
    down_ref,
    up_ref,
    dyr,
    rdy,
    lg,
    rlg,
    wsh,
    psh,
    share,
    dyp,
    tiles,
    osend,
    spread,
    base,
    acc,
    xs,
    mid,
    hs,
    rows,
    hid,
    local_sem,
    dy_s,
    dy_r,
    lg_s,
    lg_r,
    wr_s,
    wl_s,
    w_r,
    pr_s,
    pl_s,
    p_r,
    pp_s,
    pp_r,
    h1_s,
    h1_r,
    h2_s,
    h2_r,
    b_s,
    b_r,
    t_s,
    t_r,
    o_s,
    o_r,
):
    bf16 = jnp.bfloat16
    f32 = jnp.float32
    PL = G * S
    L = N // S
    R = w_ref.shape[0]
    RG = R // G
    K = dy_ref.shape[1]
    rank = pt_ref.shape[0]
    T = dy_ref.shape[0]
    C, _, RP, CD = xs.shape
    RQ = rows.shape[2]
    TL = tiles.shape[2]
    aligned = RG % 128 == 0
    pieces = L if aligned else 1
    me_g = lax.axis_index("groups")
    me = lax.axis_index("dp")
    me_z = me // S
    me_s = lax.rem(me, S)
    me_p = me_g * S + me_s

    def group_dev(k):
        return lax.rem(me + k, N)

    def plane_dev(k):
        p = lax.rem(me_p + k, PL)
        return (p // S, me_z * S + lax.rem(p, S)), p

    def line_dev(z):
        return (me_g, z * S + me_s)

    def rcopy(src, dst, ss, rs, dev):
        return pltpu.make_async_remote_copy(
            src_ref=src, dst_ref=dst, send_sem=ss, recv_sem=rs, device_id=dev, device_id_type=MESH
        )

    barrier = pltpu.get_barrier_semaphore()
    each(
        1,
        N,
        lambda k: pl.semaphore_signal(
            barrier, inc=1, device_id=(me_g, group_dev(k)), device_id_type=MESH
        ),
    )
    others = (G - 1) * S

    def greet(k):
        gg = lax.rem(me_g + 1 + k // S, G)
        pl.semaphore_signal(
            barrier, inc=1, device_id=(gg, me_z * S + lax.rem(k, S)), device_id_type=MESH
        )

    each(0, others, greet)
    dyr[...] = (
        jnp.dot(place_dy_ref[...], dy_ref[...], preferred_element_type=f32)
        .astype(bf16)
        .reshape(dyr.shape)
    )
    if aligned:
        for s in range(S):
            for z in range(L):
                start = pl.multiple_of((z * S + s) * R + me_g * RG, 128)
                share[s, :, z * RG : (z + 1) * RG] = pt_ref[:, pl.ds(start, RG)]
    else:
        share[...] = share_ref[...]
    pl.semaphore_wait(barrier, N - 1 + others)

    def dy_copy(k):
        d = group_dev(k)
        return rcopy(dyr.at[d], rdy.at[me], dy_s.at[k], dy_r.at[k], (me_g, d))

    each(1, N, lambda k: dy_copy(k).start())
    own_dy = pltpu.make_async_copy(dyr.at[me], rdy.at[me], local_sem.at[0])
    own_dy.start()

    w_part = w_ref.at[pl.ds(pl.multiple_of(me_g * RG, RG), RG)]
    own_w = pltpu.make_async_copy(w_part, wsh.at[me_z], local_sem.at[2])
    own_w.start()

    def pp_copy(k):
        s = lax.rem(me_s + k, S)
        return rcopy(
            share.at[s], psh.at[me_z, me_s], pp_s.at[k], pp_r.at[k], (me_g, me_z * S + s)
        )

    each(1, S, lambda k: pp_copy(k).start())
    own_p = pltpu.make_async_copy(share.at[me_s], psh.at[me_z, me_s], local_sem.at[3])
    own_p.start()

    def line_copies(buf, right_s, left_s, recv):
        def right(b):
            return rcopy(buf.at[b], buf.at[b], right_s.at[b], recv.at[b], line_dev(me_z + 1))

        def left(b):
            return rcopy(buf.at[b], buf.at[b], left_s.at[b], recv.at[b], line_dev(me_z - 1))

        return right, left

    def line_begin(right, left):
        @pl.when(me_z < L - 1)
        def _():
            right(me_z).start()

        @pl.when(me_z > 0)
        def _():
            left(me_z).start()

    def line_step(right, left, t):
        @pl.when(me_z - t >= 0)
        def _():
            right(me_z - t).wait_recv()

            @pl.when(me_z < L - 1)
            def _():
                right(me_z - t).start()

        @pl.when(me_z + t < L)
        def _():
            left(me_z + t).wait_recv()

            @pl.when(me_z > 0)
            def _():
                left(me_z + t).start()

    def line_end(right, left):
        def one(b):
            @pl.when(jnp.logical_and(b <= me_z, me_z < L - 1))
            def _():
                right(b).wait_send()

            @pl.when(jnp.logical_and(b >= me_z, me_z > 0))
            def _():
                left(b).wait_send()

        each(0, L, one)

    w_line = line_copies(wsh, wr_s, wl_s, w_r)
    p_line = line_copies(psh, pr_s, pl_s, p_r)

    def h1_copy(c, k):
        z = lax.rem(me_z + k, L)
        i = c * L + k
        return rcopy(xs.at[c, z], mid.at[c, me_z], h1_s.at[i], h1_r.at[i], line_dev(z))

    def own_mid(c):
        return pltpu.make_async_copy(xs.at[c, me_z], mid.at[c, me_z], local_sem.at[16 + c])

    def send_rows(c):
        start = pl.multiple_of(c * CD, CD)
        xs[c] = (
            jnp.dot(place_x_ref[...], x_ref[:, pl.ds(start, CD)], preferred_element_type=f32)
            .astype(bf16)
            .reshape(L, RP, CD)
        )
        each(1, L, lambda k: h1_copy(c, k).start())
        own_mid(c).start()

    def h2_copy(c, k):
        s = lax.rem(me_s + k, S)
        i = c * S + k
        return rcopy(
            hs.at[c, s], rows.at[c, me_s], h2_s.at[i], h2_r.at[i], (me_g, me_z * S + s)
        )

    def regroup(c):
        each(1, L, lambda k: h1_copy(c, k).wait_recv())
        own_mid(c).wait()

        def pick(s):
            q = lax.broadcasted_iota(jnp.int32, (RQ, L * RP), 0)
            j = lax.broadcasted_iota(jnp.int32, (RQ, L * RP), 1)
            hit = (j == (q // cap) * RP + s * cap + lax.rem(q, cap)) & (q < L * cap)
            sel = jnp.where(hit, 1.0, 0.0).astype(bf16)
            return jnp.dot(
                sel, mid[c].reshape(L * RP, CD), preferred_element_type=f32
            ).astype(bf16)

        def part(k):
            s = lax.rem(me_s + k, S)
            hs[c, s] = pick(s)
            h2_copy(c, k).start()

        each(1, S, part)
        rows[c, me_s] = pick(me_s)

    def b_copy(k):
        dev, _ = plane_dev(k)
        return rcopy(dy_ref, dyp.at[me_p], b_s.at[k], b_r.at[k], dev)

    each(1, PL, lambda k: b_copy(k).start())
    own_b = pltpu.make_async_copy(dy_ref, dyp.at[me_p], local_sem.at[1])
    own_b.start()
    own_w.wait()
    line_begin(*w_line)
    each(1, S, lambda k: pp_copy(k).wait_recv())
    own_p.wait()
    line_begin(*p_line)
    send_rows(0)

    each(1, N, lambda k: dy_copy(k).wait_recv())
    own_dy.wait()
    value = adapter_scale * lax.dot_general(
        rdy[...].reshape(N * ROWS, K), q_ref[...], NT, preferred_element_type=f32
    )
    lg[...] = value.astype(bf16).reshape(lg.shape)

    def lg_copy(k):
        d = group_dev(k)
        return rcopy(lg.at[d], rlg.at[me], lg_s.at[k], lg_r.at[k], (me_g, d))

    each(1, N, lambda k: lg_copy(k).start())
    own_lg = pltpu.make_async_copy(lg.at[me], rlg.at[me], local_sem.at[4])
    own_lg.start()

    def base_piece(b):
        if aligned:
            base[:, pl.ds(pl.multiple_of(b * RG, RG), RG)] = lax.dot_general(
                dyp[...].reshape(PL * T, K), wsh[b], NT, preferred_element_type=f32
            )

    each(1, PL, lambda k: b_copy(k).wait_recv())
    own_b.wait()
    base_piece(me_z)

    each(1, N, lambda k: lg_copy(k).wait_recv())
    own_lg.wait()
    tokens = jnp.dot(
        place_ref[...], rlg[...].reshape(N * ROWS, TL), preferred_element_type=f32
    )
    tiles[me_p] = tokens.astype(bf16) + hot_ref[...]

    def t_copy(k):
        dev, _ = plane_dev(k)
        return rcopy(tiles.at[me_p], tiles.at[me_p], t_s.at[k], t_r.at[k], dev)

    each(1, PL, lambda k: t_copy(k).start())

    def column(rows_of, b):
        row = lax.broadcasted_iota(jnp.int32, (TL, S * rank), 0)
        col = lax.broadcasted_iota(jnp.int32, (TL, S * rank), 1)
        hit = row == lax.rem(col, rank) if rows_of else row - rank == b * S + col // rank
        return jnp.where(hit, 1.0, 0.0).astype(bf16)

    def lora_piece(b):
        chosen = jnp.dot(
            tiles[...].reshape(PL * T, TL), column(False, b), preferred_element_type=f32
        )
        masked = (spread[...].astype(f32) * chosen).astype(bf16)
        for i in range(0, L * RG, 256):
            acc[:, i : i + 256] += jnp.dot(
                masked,
                psh[b].reshape(S * rank, L * RG)[:, i : i + 256],
                preferred_element_type=f32,
            )

    def line_use(t):
        @pl.when(me_z - t >= 0)
        def _():
            base_piece(me_z - t)
            lora_piece(me_z - t)

        @pl.when(me_z + t < L)
        def _():
            base_piece(me_z + t)
            lora_piece(me_z + t)

    acc[...] = jnp.zeros_like(acc)
    line_step(*w_line, 1)
    line_step(*p_line, 1)
    send_rows(1)
    each(1, PL, lambda k: t_copy(k).wait_recv())
    spread[...] = jnp.dot(
        tiles[...].reshape(PL * T, TL), column(True, 0), preferred_element_type=f32
    ).astype(bf16)
    lora_piece(me_z)
    line_use(1)
    if L > 2:
        line_step(*w_line, 2)
        line_step(*p_line, 2)
        send_rows(2)
        line_use(2)
    else:
        send_rows(2)

    def later(t):
        line_step(*w_line, t)
        line_step(*p_line, t)
        line_use(t)

    send_rows(3)
    regroup(0)
    each(3, L, later)
    if not aligned:
        base[...] = lax.dot_general(
            dyp[...].reshape(PL * T, K),
            wsh[...].reshape(L * RG, K),
            NT,
            preferred_element_type=f32,
        )

    def o_copy(k, i):
        dev, p = plane_dev(k)
        if not aligned:
            return rcopy(osend.at[p], out_ref.at[me_p], o_s.at[k], o_r.at[k], dev)
        start = pl.multiple_of((i * S + me_s) * R + me_g * RG, 128)
        return rcopy(
            osend.at[p, :, pl.ds(i * RG, RG)],
            out_ref.at[:, pl.ds(start, RG)],
            o_s.at[k * L + i],
            o_r.at[k * L + i],
            dev,
        )

    def own_out(i):
        if not aligned:
            return pltpu.make_async_copy(osend.at[me_p], out_ref.at[me_p], local_sem.at[8])
        start = pl.multiple_of((i * S + me_s) * R + me_g * RG, 128)
        return pltpu.make_async_copy(
            osend.at[me_p, :, pl.ds(i * RG, RG)],
            out_ref.at[:, pl.ds(start, RG)],
            local_sem.at[8 + i],
        )

    def block(k):
        p = lax.rem(me_p + k, PL)
        at = pl.ds(pl.multiple_of(p * T, T), T)
        term = acc[at].astype(bf16).astype(f32)
        osend[p] = (base[at] + term).astype(bf16)

    def block_and_send(k):
        block(k)
        for i in range(pieces):
            o_copy(k, i).start()

    each(1, PL, block_and_send)
    block(0)
    for i in range(pieces):
        own_out(i).start()

    q = lax.broadcasted_iota(jnp.int32, (S * RQ, N * ROWS), 0)
    j = lax.broadcasted_iota(jnp.int32, (S * RQ, N * ROWS), 1)
    inside = lax.rem(q, RQ)
    slot = ((inside // cap) * S + q // RQ) * ROWS + lax.rem(inside, cap)
    sel = jnp.where((j == slot) & (inside < L * cap), 1.0, 0.0).astype(bf16)
    lora = jnp.dot(sel, lg[...].reshape(N * ROWS, TL), preferred_element_type=f32).astype(bf16)
    grad = jnp.dot(sel, rdy[...].reshape(N * ROWS, K), preferred_element_type=f32).astype(bf16)

    hid[...] = jnp.zeros_like(hid)
    each(1, C, regroup)

    def finish(c):
        each(1, S, lambda k: h2_copy(c, k).wait_recv())
        start = pl.multiple_of(c * CD, CD)
        rc = rows[c].reshape(S * RQ, CD)
        hid[...] += lax.dot_general(
            rc, pt_ref[:, pl.ds(start, CD)], NT, preferred_element_type=f32
        )
        down_ref[:, pl.ds(start, CD)] = lax.dot_general(
            lora, rc, TN, preferred_element_type=f32
        )[:rank]

    each(0, C, finish)
    up_ref[...] = adapter_scale * lax.dot_general(
        hid[...].astype(bf16), grad, TN, preferred_element_type=f32
    )

    for i in range(pieces):
        each(1, PL, lambda k: o_copy(k, i).wait_recv())
        own_out(i).wait()
    each(1, N, lambda k: dy_copy(k).wait_send())
    each(1, N, lambda k: lg_copy(k).wait_send())
    each(1, S, lambda k: pp_copy(k).wait_send())
    for c in range(C):
        each(1, L, lambda k: h1_copy(c, k).wait_send())
        each(1, S, lambda k: h2_copy(c, k).wait_send())
    line_end(*w_line)
    line_end(*p_line)
    each(1, PL, lambda k: b_copy(k).wait_send())
    each(1, PL, lambda k: t_copy(k).wait_send())
    for i in range(pieces):
        each(1, PL, lambda k: o_copy(k, i).wait_send())


def per_device(
    G,
    inputs,
    output_gradient,
    token_adapter_index,
    owner_index_map,
    frozen_key_weight,
    down_panels,
    up_panels,
):
    N = lax.axis_size("dp")
    S = max(1, 8 // G)
    L = N // S
    PL = G * S
    T, D = inputs.shape
    K = output_gradient.shape[1]
    R = frozen_key_weight.shape[0]
    RG = R // G
    rank = down_panels.shape[2]
    cap = max(2, 3 * T // (2 * N))
    TL = -(-(rank + N) // 128) * 128
    RP = ceil16(S * cap)
    RQ = ceil16(L * cap)
    C = CHUNKS
    CD = D // C
    aligned = RG % 128 == 0
    pieces = L if aligned else 1
    bf16 = jnp.bfloat16
    f32 = jnp.float32

    index = token_adapter_index[:, 0]
    hot = index[:, None] == jnp.arange(N, dtype=jnp.int32)[None, :]
    before = jnp.arange(T)[:, None] > jnp.arange(T)[None, :]
    earlier = jnp.dot(before.astype(bf16), hot.astype(bf16), preferred_element_type=f32)
    turn = jnp.sum(jnp.where(hot, earlier, 0.0), axis=1).astype(jnp.int32)
    owner = jnp.sum(jnp.where(hot, owner_index_map[None, :], 0), axis=1)

    def numbers(n):
        return jnp.arange(n, dtype=jnp.int32)

    x_slot = (owner // S) * RP + (owner % S) * cap + turn
    place_x = (numbers(L * RP)[:, None] == x_slot[None, :]).astype(bf16)
    slot = owner * ROWS + turn
    place_dy = (numbers(N * ROWS)[:, None] == slot[None, :]).astype(bf16)
    place_t = (slot[:, None] == numbers(N * ROWS)[None, :]).astype(bf16)
    owner_hot = (owner[:, None] == numbers(TL)[None, :] - rank).astype(bf16)

    turned = down_panels[0].T
    if aligned:
        shares = turned
    else:
        group = lax.axis_index("groups")
        mine = lax.dynamic_index_in_dim(
            turned.reshape(rank, L, S, G, RG), group, 3, keepdims=False
        )
        shares = mine.transpose(2, 0, 1, 3).reshape(S, rank, L * RG)
    up_padded = jnp.pad(up_panels[0], ((0, TL - rank), (0, 0)))

    anyspace = pl.BlockSpec(memory_space=pl.ANY)
    vmem = pl.BlockSpec(memory_space=pltpu.VMEM)
    dma = pltpu.SemaphoreType.DMA
    out_shape = (T, D) if aligned else (PL, T, L * RG)
    outs, down, up = pl.pallas_call(
        functools.partial(exchange_kernel, G, S, N, cap),
        out_shape=(
            jax.ShapeDtypeStruct(out_shape, bf16),
            jax.ShapeDtypeStruct((rank, D), f32),
            jax.ShapeDtypeStruct((rank, K), f32),
        ),
        in_specs=[
            vmem,
            vmem,
            anyspace,
            vmem,
            anyspace if aligned else vmem,
            vmem,
            vmem,
            vmem,
            vmem,
            vmem,
        ],
        out_specs=[anyspace, vmem, vmem],
        scratch_shapes=[
            pltpu.VMEM((N, ROWS, K), bf16),
            pltpu.VMEM((N, ROWS, K), bf16),
            pltpu.VMEM((N, ROWS, TL), bf16),
            pltpu.VMEM((N, ROWS, TL), bf16),
            pltpu.VMEM((L, RG, K), bf16),
            pltpu.VMEM((L, S, rank, L * RG), bf16),
            pltpu.VMEM((S, rank, L * RG), bf16),
            pltpu.VMEM((PL, T, K), bf16),
            pltpu.VMEM((PL, T, TL), bf16),
            pltpu.VMEM((PL, T, L * RG), bf16),
            pltpu.VMEM((PL * T, S * rank), bf16),
            pltpu.VMEM((PL * T, L * RG), f32),
            pltpu.VMEM((PL * T, L * RG), f32),
            pltpu.VMEM((C, L, RP, CD), bf16),
            pltpu.VMEM((C, L, RP, CD), bf16),
            pltpu.VMEM((C, S, RQ, CD), bf16),
            pltpu.VMEM((C, S, RQ, CD), bf16),
            pltpu.VMEM((S * RQ, rank), f32),
            dma((16 + C,)),
        ]
        + [dma((N,))] * 4
        + [dma((L,))] * 6
        + [dma((S,))] * 2
        + [dma((C * L,))] * 2
        + [dma((C * S,))] * 2
        + [dma((PL,))] * 4
        + [dma((PL * pieces,))] * 2,
        compiler_params=pltpu.CompilerParams(
            collective_id=0, has_side_effects=True, vmem_limit_bytes=58 * 1024 * 1024
        ),
        cost_estimate=pl.CostEstimate(
            flops=4 * PL * T * L * RG * K, bytes_accessed=16 * 1024 * 1024, transcendentals=0
        ),
        name="exchange",
    )(
        inputs,
        output_gradient,
        frozen_key_weight,
        turned,
        shares,
        place_x,
        place_dy,
        place_t,
        owner_hot,
        up_padded,
    )

    if not aligned:
        outs = outs.reshape(G, S, T, L, RG).transpose(2, 3, 1, 0, 4).reshape(T, D)
    return (outs, down.T[None], up[None])


def solution(mesh):
    in_specs = (
        P(("groups", "dp"), None),
        P(("groups", "dp"), None),
        P(("groups", "dp"), None),
        P(),
        P("dp", None),
        P("dp", None, None),
        P("dp", None, None),
    )
    out_specs = (
        P(("groups", "dp"), None),
        P(("groups", "dp"), None, None),
        P(("groups", "dp"), None, None),
    )
    return jax.shard_map(
        functools.partial(per_device, mesh.shape["groups"]),
        mesh=mesh,
        in_specs=in_specs,
        out_specs=out_specs,
        check_vma=False,
    )
```

```python
import functools

import jax
import jax.numpy as jnp
from jax import lax
from jax.experimental import pallas as pl
from jax.experimental.pallas import tpu as pltpu
from jax.sharding import PartitionSpec as P

adapter_scale = 2.0
MESH = pl.DeviceIdType.MESH
ROWS = 16
CHUNKS = 4
NT = (((1,), (1,)), ((), ()))
TN = (((0,), (0,)), ((), ()))


def ceil16(n):
    return -(-n // 16) * 16


def each(lo, hi, body):
    def step(k, c):
        body(k)
        return c

    lax.fori_loop(lo, hi, step, 0)


def exchange_kernel(
    G,
    S,
    N,
    cap,
    x_ref,
    dy_ref,
    w_ref,
    pt_ref,
    share_ref,
    place_x_ref,
    place_dy_ref,
    place_ref,
    hot_ref,
    q_ref,
    out_ref,
    down_ref,
    up_ref,
    dyr,
    rdy,
    lg,
    rlg,
    wsh,
    psh,
    share,
    dyp,
    tiles,
    osend,
    spread,
    base,
    acc,
    xs,
    mid,
    hs,
    rows,
    hid,
    local_sem,
    dy_s,
    dy_r,
    lg_s,
    lg_r,
    wr_s,
    wl_s,
    w_r,
    pr_s,
    pl_s,
    p_r,
    pp_s,
    pp_r,
    h1_s,
    h1_r,
    h2_s,
    h2_r,
    b_s,
    b_r,
    t_s,
    t_r,
    o_s,
    o_r,
):
    bf16 = jnp.bfloat16
    f32 = jnp.float32
    PL = G * S
    L = N // S
    R = w_ref.shape[0]
    RG = R // G
    K = dy_ref.shape[1]
    rank = pt_ref.shape[0]
    T = dy_ref.shape[0]
    C, _, RP, CD = xs.shape
    RQ = rows.shape[2]
    TL = tiles.shape[2]
    aligned = RG % 128 == 0
    pieces = L if aligned else 1
    me_g = lax.axis_index("groups")
    me = lax.axis_index("dp")
    me_z = me // S
    me_s = lax.rem(me, S)
    me_p = me_g * S + me_s

    def group_dev(k):
        return lax.rem(me + k, N)

    def plane_dev(k):
        p = lax.rem(me_p + k, PL)
        return (p // S, me_z * S + lax.rem(p, S)), p

    def line_dev(z):
        return (me_g, z * S + me_s)

    def rcopy(src, dst, ss, rs, dev):
        return pltpu.make_async_remote_copy(
            src_ref=src, dst_ref=dst, send_sem=ss, recv_sem=rs, device_id=dev, device_id_type=MESH
        )

    barrier = pltpu.get_barrier_semaphore()
    each(
        1,
        N,
        lambda k: pl.semaphore_signal(
            barrier, inc=1, device_id=(me_g, group_dev(k)), device_id_type=MESH
        ),
    )
    others = (G - 1) * S

    def greet(k):
        gg = lax.rem(me_g + 1 + k // S, G)
        pl.semaphore_signal(
            barrier, inc=1, device_id=(gg, me_z * S + lax.rem(k, S)), device_id_type=MESH
        )

    each(0, others, greet)
    dyr[...] = (
        jnp.dot(place_dy_ref[...], dy_ref[...], preferred_element_type=f32)
        .astype(bf16)
        .reshape(dyr.shape)
    )
    if aligned:
        for s in range(S):
            for z in range(L):
                start = pl.multiple_of((z * S + s) * R + me_g * RG, 128)
                share[s, :, z * RG : (z + 1) * RG] = pt_ref[:, pl.ds(start, RG)]
    else:
        share[...] = share_ref[...]
    pl.semaphore_wait(barrier, N - 1 + others)

    def dy_copy(k):
        d = group_dev(k)
        return rcopy(dyr.at[d], rdy.at[me], dy_s.at[k], dy_r.at[k], (me_g, d))

    each(1, N, lambda k: dy_copy(k).start())
    own_dy = pltpu.make_async_copy(dyr.at[me], rdy.at[me], local_sem.at[0])
    own_dy.start()

    w_part = w_ref.at[pl.ds(pl.multiple_of(me_g * RG, RG), RG)]
    own_w = pltpu.make_async_copy(w_part, wsh.at[me_z], local_sem.at[2])
    own_w.start()

    def pp_copy(k):
        s = lax.rem(me_s + k, S)
        return rcopy(
            share.at[s], psh.at[me_z, me_s], pp_s.at[k], pp_r.at[k], (me_g, me_z * S + s)
        )

    each(1, S, lambda k: pp_copy(k).start())
    own_p = pltpu.make_async_copy(share.at[me_s], psh.at[me_z, me_s], local_sem.at[3])
    own_p.start()

    def line_copies(buf, right_s, left_s, recv):
        def right(b):
            return rcopy(buf.at[b], buf.at[b], right_s.at[b], recv.at[b], line_dev(me_z + 1))

        def left(b):
            return rcopy(buf.at[b], buf.at[b], left_s.at[b], recv.at[b], line_dev(me_z - 1))

        return right, left

    def line_begin(right, left):
        @pl.when(me_z < L - 1)
        def _():
            right(me_z).start()

        @pl.when(me_z > 0)
        def _():
            left(me_z).start()

    def line_step(right, left, t):
        @pl.when(me_z - t >= 0)
        def _():
            right(me_z - t).wait_recv()

            @pl.when(me_z < L - 1)
            def _():
                right(me_z - t).start()

        @pl.when(me_z + t < L)
        def _():
            left(me_z + t).wait_recv()

            @pl.when(me_z > 0)
            def _():
                left(me_z + t).start()

    def line_end(right, left):
        def one(b):
            @pl.when(jnp.logical_and(b <= me_z, me_z < L - 1))
            def _():
                right(b).wait_send()

            @pl.when(jnp.logical_and(b >= me_z, me_z > 0))
            def _():
                left(b).wait_send()

        each(0, L, one)

    w_line = line_copies(wsh, wr_s, wl_s, w_r)
    p_line = line_copies(psh, pr_s, pl_s, p_r)

    def h1_copy(c, k):
        z = lax.rem(me_z + k, L)
        i = c * L + k
        return rcopy(xs.at[c, z], mid.at[c, me_z], h1_s.at[i], h1_r.at[i], line_dev(z))

    def own_mid(c):
        return pltpu.make_async_copy(xs.at[c, me_z], mid.at[c, me_z], local_sem.at[16 + c])

    def send_rows(c):
        start = pl.multiple_of(c * CD, CD)
        xs[c] = (
            jnp.dot(place_x_ref[...], x_ref[:, pl.ds(start, CD)], preferred_element_type=f32)
            .astype(bf16)
            .reshape(L, RP, CD)
        )
        each(1, L, lambda k: h1_copy(c, k).start())
        own_mid(c).start()

    def h2_copy(c, k):
        s = lax.rem(me_s + k, S)
        i = c * S + k
        return rcopy(
            hs.at[c, s], rows.at[c, me_s], h2_s.at[i], h2_r.at[i], (me_g, me_z * S + s)
        )

    def regroup(c):
        each(1, L, lambda k: h1_copy(c, k).wait_recv())
        own_mid(c).wait()

        def pick(s):
            q = lax.broadcasted_iota(jnp.int32, (RQ, L * RP), 0)
            j = lax.broadcasted_iota(jnp.int32, (RQ, L * RP), 1)
            hit = (j == (q // cap) * RP + s * cap + lax.rem(q, cap)) & (q < L * cap)
            sel = jnp.where(hit, 1.0, 0.0).astype(bf16)
            return jnp.dot(
                sel, mid[c].reshape(L * RP, CD), preferred_element_type=f32
            ).astype(bf16)

        def part(k):
            s = lax.rem(me_s + k, S)
            hs[c, s] = pick(s)
            h2_copy(c, k).start()

        each(1, S, part)
        rows[c, me_s] = pick(me_s)

    def b_copy(k):
        dev, _ = plane_dev(k)
        return rcopy(dy_ref, dyp.at[me_p], b_s.at[k], b_r.at[k], dev)

    each(1, PL, lambda k: b_copy(k).start())
    own_b = pltpu.make_async_copy(dy_ref, dyp.at[me_p], local_sem.at[1])
    own_b.start()
    own_w.wait()
    line_begin(*w_line)
    each(1, S, lambda k: pp_copy(k).wait_recv())
    own_p.wait()
    line_begin(*p_line)
    send_rows(0)

    each(1, N, lambda k: dy_copy(k).wait_recv())
    own_dy.wait()
    value = adapter_scale * lax.dot_general(
        rdy[...].reshape(N * ROWS, K), q_ref[...], NT, preferred_element_type=f32
    )
    lg[...] = value.astype(bf16).reshape(lg.shape)

    def lg_copy(k):
        d = group_dev(k)
        return rcopy(lg.at[d], rlg.at[me], lg_s.at[k], lg_r.at[k], (me_g, d))

    each(1, N, lambda k: lg_copy(k).start())
    own_lg = pltpu.make_async_copy(lg.at[me], rlg.at[me], local_sem.at[4])
    own_lg.start()

    def base_piece(b):
        if aligned:
            base[:, pl.ds(pl.multiple_of(b * RG, RG), RG)] = lax.dot_general(
                dyp[...].reshape(PL * T, K), wsh[b], NT, preferred_element_type=f32
            )

    send_rows(1)
    line_step(*w_line, 1)
    line_step(*p_line, 1)

    each(1, N, lambda k: lg_copy(k).wait_recv())
    own_lg.wait()
    tokens = jnp.dot(
        place_ref[...], rlg[...].reshape(N * ROWS, TL), preferred_element_type=f32
    )
    tiles[me_p] = tokens.astype(bf16) + hot_ref[...]

    def t_copy(k):
        dev, _ = plane_dev(k)
        return rcopy(tiles.at[me_p], tiles.at[me_p], t_s.at[k], t_r.at[k], dev)

    each(1, PL, lambda k: t_copy(k).start())

    def column(rows_of, b):
        row = lax.broadcasted_iota(jnp.int32, (TL, S * rank), 0)
        col = lax.broadcasted_iota(jnp.int32, (TL, S * rank), 1)
        hit = row == lax.rem(col, rank) if rows_of else row - rank == b * S + col // rank
        return jnp.where(hit, 1.0, 0.0).astype(bf16)

    def lora_piece(b):
        chosen = jnp.dot(
            tiles[...].reshape(PL * T, TL), column(False, b), preferred_element_type=f32
        )
        masked = (spread[...].astype(f32) * chosen).astype(bf16)
        for i in range(0, L * RG, 256):
            acc[:, i : i + 256] += jnp.dot(
                masked,
                psh[b].reshape(S * rank, L * RG)[:, i : i + 256],
                preferred_element_type=f32,
            )

    def line_use(t):
        @pl.when(me_z - t >= 0)
        def _():
            base_piece(me_z - t)
            lora_piece(me_z - t)

        @pl.when(me_z + t < L)
        def _():
            base_piece(me_z + t)
            lora_piece(me_z + t)

    send_rows(2)
    acc[...] = jnp.zeros_like(acc)
    each(1, PL, lambda k: b_copy(k).wait_recv())
    own_b.wait()
    base_piece(me_z)
    if L > 2:
        line_step(*w_line, 2)
        line_step(*p_line, 2)
    send_rows(3)
    each(1, PL, lambda k: t_copy(k).wait_recv())
    spread[...] = jnp.dot(
        tiles[...].reshape(PL * T, TL), column(True, 0), preferred_element_type=f32
    ).astype(bf16)
    lora_piece(me_z)
    line_use(1)
    if L > 2:
        line_use(2)

    def later(t):
        line_step(*w_line, t)
        line_step(*p_line, t)
        line_use(t)

    regroup(0)
    each(3, L, later)
    if not aligned:
        base[...] = lax.dot_general(
            dyp[...].reshape(PL * T, K),
            wsh[...].reshape(L * RG, K),
            NT,
            preferred_element_type=f32,
        )

    def o_copy(k, i):
        dev, p = plane_dev(k)
        if not aligned:
            return rcopy(osend.at[p], out_ref.at[me_p], o_s.at[k], o_r.at[k], dev)
        start = pl.multiple_of((i * S + me_s) * R + me_g * RG, 128)
        return rcopy(
            osend.at[p, :, pl.ds(i * RG, RG)],
            out_ref.at[:, pl.ds(start, RG)],
            o_s.at[k * L + i],
            o_r.at[k * L + i],
            dev,
        )

    def own_out(i):
        if not aligned:
            return pltpu.make_async_copy(osend.at[me_p], out_ref.at[me_p], local_sem.at[8])
        start = pl.multiple_of((i * S + me_s) * R + me_g * RG, 128)
        return pltpu.make_async_copy(
            osend.at[me_p, :, pl.ds(i * RG, RG)],
            out_ref.at[:, pl.ds(start, RG)],
            local_sem.at[8 + i],
        )

    def block(k):
        p = lax.rem(me_p + k, PL)
        at = pl.ds(pl.multiple_of(p * T, T), T)
        term = acc[at].astype(bf16).astype(f32)
        osend[p] = (base[at] + term).astype(bf16)

    def block_and_send(k):
        block(k)
        for i in range(pieces):
            o_copy(k, i).start()

    each(1, PL, block_and_send)
    block(0)
    for i in range(pieces):
        own_out(i).start()

    q = lax.broadcasted_iota(jnp.int32, (S * RQ, N * ROWS), 0)
    j = lax.broadcasted_iota(jnp.int32, (S * RQ, N * ROWS), 1)
    inside = lax.rem(q, RQ)
    slot = ((inside // cap) * S + q // RQ) * ROWS + lax.rem(inside, cap)
    sel = jnp.where((j == slot) & (inside < L * cap), 1.0, 0.0).astype(bf16)
    lora = jnp.dot(sel, lg[...].reshape(N * ROWS, TL), preferred_element_type=f32).astype(bf16)
    grad = jnp.dot(sel, rdy[...].reshape(N * ROWS, K), preferred_element_type=f32).astype(bf16)

    hid[...] = jnp.zeros_like(hid)
    each(1, C, regroup)

    def finish(c):
        each(1, S, lambda k: h2_copy(c, k).wait_recv())
        start = pl.multiple_of(c * CD, CD)
        rc = rows[c].reshape(S * RQ, CD)
        hid[...] += lax.dot_general(
            rc, pt_ref[:, pl.ds(start, CD)], NT, preferred_element_type=f32
        )
        down_ref[:, pl.ds(start, CD)] = lax.dot_general(
            lora, rc, TN, preferred_element_type=f32
        )[:rank]

    each(0, C, finish)
    up_ref[...] = adapter_scale * lax.dot_general(
        hid[...].astype(bf16), grad, TN, preferred_element_type=f32
    )

    for i in range(pieces):
        each(1, PL, lambda k: o_copy(k, i).wait_recv())
        own_out(i).wait()
    each(1, N, lambda k: dy_copy(k).wait_send())
    each(1, N, lambda k: lg_copy(k).wait_send())
    each(1, S, lambda k: pp_copy(k).wait_send())
    for c in range(C):
        each(1, L, lambda k: h1_copy(c, k).wait_send())
        each(1, S, lambda k: h2_copy(c, k).wait_send())
    line_end(*w_line)
    line_end(*p_line)
    each(1, PL, lambda k: b_copy(k).wait_send())
    each(1, PL, lambda k: t_copy(k).wait_send())
    for i in range(pieces):
        each(1, PL, lambda k: o_copy(k, i).wait_send())


def per_device(
    G,
    inputs,
    output_gradient,
    token_adapter_index,
    owner_index_map,
    frozen_key_weight,
    down_panels,
    up_panels,
):
    N = lax.axis_size("dp")
    S = max(1, 8 // G)
    L = N // S
    PL = G * S
    T, D = inputs.shape
    K = output_gradient.shape[1]
    R = frozen_key_weight.shape[0]
    RG = R // G
    rank = down_panels.shape[2]
    cap = max(2, 3 * T // (2 * N))
    TL = -(-(rank + N) // 128) * 128
    RP = ceil16(S * cap)
    RQ = ceil16(L * cap)
    C = CHUNKS
    CD = D // C
    aligned = RG % 128 == 0
    pieces = L if aligned else 1
    bf16 = jnp.bfloat16
    f32 = jnp.float32

    index = token_adapter_index[:, 0]
    hot = index[:, None] == jnp.arange(N, dtype=jnp.int32)[None, :]
    before = jnp.arange(T)[:, None] > jnp.arange(T)[None, :]
    earlier = jnp.dot(before.astype(bf16), hot.astype(bf16), preferred_element_type=f32)
    turn = jnp.sum(jnp.where(hot, earlier, 0.0), axis=1).astype(jnp.int32)
    owner = jnp.sum(jnp.where(hot, owner_index_map[None, :], 0), axis=1)

    def numbers(n):
        return jnp.arange(n, dtype=jnp.int32)

    x_slot = (owner // S) * RP + (owner % S) * cap + turn
    place_x = (numbers(L * RP)[:, None] == x_slot[None, :]).astype(bf16)
    slot = owner * ROWS + turn
    place_dy = (numbers(N * ROWS)[:, None] == slot[None, :]).astype(bf16)
    place_t = (slot[:, None] == numbers(N * ROWS)[None, :]).astype(bf16)
    owner_hot = (owner[:, None] == numbers(TL)[None, :] - rank).astype(bf16)

    turned = down_panels[0].T
    if aligned:
        shares = turned
    else:
        group = lax.axis_index("groups")
        mine = lax.dynamic_index_in_dim(
            turned.reshape(rank, L, S, G, RG), group, 3, keepdims=False
        )
        shares = mine.transpose(2, 0, 1, 3).reshape(S, rank, L * RG)
    up_padded = jnp.pad(up_panels[0], ((0, TL - rank), (0, 0)))

    anyspace = pl.BlockSpec(memory_space=pl.ANY)
    vmem = pl.BlockSpec(memory_space=pltpu.VMEM)
    dma = pltpu.SemaphoreType.DMA
    out_shape = (T, D) if aligned else (PL, T, L * RG)
    outs, down, up = pl.pallas_call(
        functools.partial(exchange_kernel, G, S, N, cap),
        out_shape=(
            jax.ShapeDtypeStruct(out_shape, bf16),
            jax.ShapeDtypeStruct((rank, D), f32),
            jax.ShapeDtypeStruct((rank, K), f32),
        ),
        in_specs=[
            vmem,
            vmem,
            anyspace,
            vmem,
            anyspace if aligned else vmem,
            vmem,
            vmem,
            vmem,
            vmem,
            vmem,
        ],
        out_specs=[anyspace, vmem, vmem],
        scratch_shapes=[
            pltpu.VMEM((N, ROWS, K), bf16),
            pltpu.VMEM((N, ROWS, K), bf16),
            pltpu.VMEM((N, ROWS, TL), bf16),
            pltpu.VMEM((N, ROWS, TL), bf16),
            pltpu.VMEM((L, RG, K), bf16),
            pltpu.VMEM((L, S, rank, L * RG), bf16),
            pltpu.VMEM((S, rank, L * RG), bf16),
            pltpu.VMEM((PL, T, K), bf16),
            pltpu.VMEM((PL, T, TL), bf16),
            pltpu.VMEM((PL, T, L * RG), bf16),
            pltpu.VMEM((PL * T, S * rank), bf16),
            pltpu.VMEM((PL * T, L * RG), f32),
            pltpu.VMEM((PL * T, L * RG), f32),
            pltpu.VMEM((C, L, RP, CD), bf16),
            pltpu.VMEM((C, L, RP, CD), bf16),
            pltpu.VMEM((C, S, RQ, CD), bf16),
            pltpu.VMEM((C, S, RQ, CD), bf16),
            pltpu.VMEM((S * RQ, rank), f32),
            dma((16 + C,)),
        ]
        + [dma((N,))] * 4
        + [dma((L,))] * 6
        + [dma((S,))] * 2
        + [dma((C * L,))] * 2
        + [dma((C * S,))] * 2
        + [dma((PL,))] * 4
        + [dma((PL * pieces,))] * 2,
        compiler_params=pltpu.CompilerParams(
            collective_id=0, has_side_effects=True, vmem_limit_bytes=58 * 1024 * 1024
        ),
        cost_estimate=pl.CostEstimate(
            flops=4 * PL * T * L * RG * K, bytes_accessed=16 * 1024 * 1024, transcendentals=0
        ),
        name="exchange",
    )(
        inputs,
        output_gradient,
        frozen_key_weight,
        turned,
        shares,
        place_x,
        place_dy,
        place_t,
        owner_hot,
        up_padded,
    )

    if not aligned:
        outs = outs.reshape(G, S, T, L, RG).transpose(2, 3, 1, 0, 4).reshape(T, D)
    return (outs, down.T[None], up[None])


def solution(mesh):
    in_specs = (
        P(("groups", "dp"), None),
        P(("groups", "dp"), None),
        P(("groups", "dp"), None),
        P(),
        P("dp", None),
        P("dp", None, None),
        P("dp", None, None),
    )
    out_specs = (
        P(("groups", "dp"), None),
        P(("groups", "dp"), None, None),
        P(("groups", "dp"), None, None),
    )
    return jax.shard_map(
        functools.partial(per_device, mesh.shape["groups"]),
        mesh=mesh,
        in_specs=in_specs,
        out_specs=out_specs,
        check_vma=False,
    )
```
